1024 devices in a mesh: dp: 32 (over z), ctx: 16 (over x, y), tp: 2 (over core).
Axes of the slice: x: 4, y: 4, z: 32, core: 2. Of those that a mesh axis runs over, the one named last changes fastest.
Arguments:
- cotangent: bfloat16 [2048, 3072], P(('dp', 'ctx'), 'tp'), may hold values from -6 to 6
- expert_ids: int32 [2048, 2], P(('dp', 'ctx')), may hold values from 0 to 7, all different within a row; in each aligned block of 64 rows (0 to 63, 64 to 127, ...) at most 32 rows name the same one
- route_probs: bfloat16 [2048, 2], P(('dp', 'ctx')), may hold values from 0.099609375 to 1
- saved_gate: bfloat16 [1024, 131072], P(None, ('dp', 'ctx')), may hold values from -6 to 6
- saved_up: bfloat16 [1024, 131072], P(None, ('dp', 'ctx')), may hold values from -6 to 6
- down_weight: bfloat16 [131072, 3072], P(('dp', 'ctx'), 'tp'), may hold values from -0.046875 to 0.046875
Outputs:
- grad_gate: bfloat16 [1024, 131072], P(None, ('dp', 'ctx'))
- grad_up: bfloat16 [1024, 131072], P(None, ('dp', 'ctx'))
- grad_down: bfloat16 [131072, 3072], P(('dp', 'ctx'), 'tp')
The draws below stay inside these ranges and needn't reach their ends.
Inputs may be any that keep to these rules, and one draw needn't show every extreme that they name: `expert_ids`: the two experts of a token differ. In each aligned block of 64 rows (the tokens of one index of dp), no expert is named by more than 32 rows, a bound that some block reaches.
All inputs are finite; a program needn't handle non-finite values.
Results may differ from the reference program's by a relative error of at most 0.0057.
Values may be sent and summed in bfloat16 or wider, within the bound.
A program may use at most 64 MiB of HBM per device.

```python
import math
import jax
import jax.numpy as jnp
import numpy as np
from jax import lax

D = 3072
FF = 16384
EXPERTS = 8
TOP = 2
TOK_DEV = 4
CAPR = 32
SLOTS = 1024
TOKENS = 2048
N_DP = 32
N_CTX = 16


def steps_of(key, extent, cuts, smallest, largest):
    def one(dim, parts):
        heights = jax.random.uniform(jax.random.fold_in(jax.random.fold_in(key, 6), dim), (parts,), jnp.float32, smallest / len(cuts), largest / len(cuts))
        return jnp.repeat(jnp.exp(heights), extent[dim] // parts).reshape((-1,) + (1,) * (len(extent) - dim - 1))

    gain = one(*cuts[0])
    for cut in cuts[1:]:
        gain = gain * one(*cut)
    return gain


def deal_out(own_key, own, number, rows, amount, top, reach, slope):
    sequence = jax.random.permutation(own_key, amount)
    heavy_load, usual = portions_of(amount, rows * top, reach, slope, True), portions_of(amount, rows * top, reach, slope, False)
    places = jnp.arange(amount)

    def named(sizes, rotation):
        used = int((sizes > 0).sum())
        fixed = max(1, used // 4)
        passed = fixed + (places - fixed + rotation * (used - fixed)) % max(1, amount - fixed)
        return jnp.zeros((amount,), jnp.int32).at[sequence[jnp.where(places < fixed, places, passed)]].set(jnp.asarray(sizes, jnp.int32))

    sizes = jnp.where(number % 4 == 0, named(heavy_load, number // 4), named(usual, number - number // 4 - 1))
    mixed = jax.random.permutation(jax.random.fold_in(own, 3), amount)
    donor, taker = mixed[0:amount // 2 * 2:2], mixed[1:amount // 2 * 2:2]
    margin = jnp.minimum(sizes[donor] - 1, reach - sizes[taker]) // 2
    margin = jnp.where((donor == sequence[0]) | (taker == sequence[0]) | (sizes[taker] == 0), 0, jnp.maximum(margin, 0))
    passed = jax.random.randint(jax.random.fold_in(own, 4), (amount // 2,), 0, 1 << 20) % (margin + 1)
    sizes = sizes.at[donor].add(-passed).at[taker].add(passed)
    labels = jnp.searchsorted(jnp.cumsum(sizes), jnp.arange(rows * top), side="right").astype(jnp.int32)
    table = labels.reshape(top, rows).T
    table = table[jax.random.permutation(jax.random.fold_in(own, 1), rows)]
    rotation = jax.random.randint(jax.random.fold_in(own, 2), (rows, 1), 0, top)
    return jnp.take_along_axis(table, (jnp.arange(top)[None, :] + rotation) % top, axis=1)


def portions_of(number_of, total, bound, slope, full):
    loads = [(1 << 20) // math.isqrt(standing ** slope) + 1 for standing in range(1, number_of + 1)]
    largest = bound if full else min(bound, max(-(-total // number_of), total * loads[0] // sum(loads)))
    least = 1 if total - largest >= number_of - 1 else 0
    holding, spare = [largest] + [least] * (number_of - 1), total - largest - least * (number_of - 1)
    while spare > 0:
        free = [i for i in range(1, number_of) if holding[i] < largest] or [i for i in range(1, number_of) if holding[i] < bound]
        mass, left = sum([loads[i] for i in free]), spare
        for i in free:
            addition = min(bound - holding[i], max(1, left * loads[i] // mass), spare)
            holding[i] = holding[i] + addition
            spare = spare - addition
    return np.array(holding)


def normal_values(stream_key, extent, width, reach, split=(), kind=jnp.bfloat16):
    level = steps_of(stream_key, extent, split, -0.22, 0.18) if split else 1.0
    entries = jax.random.normal(stream_key, extent, jnp.float32) * width * level
    return jnp.minimum(jnp.maximum(entries, -reach), reach).astype(kind)


def setup_inputs(seed: int = 0) -> dict:
    key_of = jax.random.split(jax.random.key(seed), 7)
    cotangent = normal_values(key_of[0], (TOKENS, D), 1.0, 6.0, ((0, 512), (1, 2)))
    expert_ids_keys = jax.random.split(jax.random.fold_in(key_of[1], 1), TOKENS // (N_CTX * TOK_DEV))
    expert_ids_turns = jax.random.permutation(jax.random.fold_in(key_of[1], 3), TOKENS // (N_CTX * TOK_DEV))
    expert_ids = jax.vmap(lambda own, number: deal_out(jax.random.fold_in(key_of[1], 2), own, number, N_CTX * TOK_DEV, EXPERTS, TOP, CAPR, 2))(expert_ids_keys, expert_ids_turns).reshape((TOKENS, TOP))
    route_probs = jnp.clip(0.099609375 + 0.9003906 * jax.random.uniform(key_of[2], (TOKENS, TOP), jnp.float32) ** steps_of(key_of[2], (TOKENS, TOP), ((0, 512),), -0.2, 0.2), 0.099609375, 1.0).astype(jnp.bfloat16)
    saved_gate = normal_values(key_of[3], (SLOTS, EXPERTS * FF), 1.5, 6.0, ((1, 512),))
    saved_up = normal_values(key_of[4], (SLOTS, EXPERTS * FF), 1.0, 6.0, ((1, 512),))
    down_weight = normal_values(key_of[5], (EXPERTS * FF, D), FF ** -0.5, 0.046875, ((0, 512), (1, 2)))
    return {"cotangent": cotangent, "expert_ids": expert_ids, "route_probs": route_probs, "saved_gate": saved_gate, "saved_up": saved_up, "down_weight": down_weight}


def routed_rows(cotangent, expert_ids, route_probs):
    block_rows = N_CTX * TOK_DEV
    flat_ids = expert_ids.reshape(N_DP, block_rows * TOP)
    flat_probs = route_probs.reshape(N_DP, block_rows * TOP).astype(jnp.float32)
    hits = (flat_ids[:, :, None] == jnp.arange(EXPERTS, dtype=jnp.int32)[None, None, :]).astype(jnp.int32)
    earlier = jnp.cumsum(hits, axis=1) - hits
    slot = jnp.sum(earlier * hits, axis=2)
    at_slot = (slot[:, :, None] == jnp.arange(CAPR, dtype=jnp.int32)[None, None, :]).astype(jnp.float32)
    weights = hits.astype(jnp.float32)[:, :, :, None] * at_slot[:, :, None, :] * flat_probs[:, :, None, None]
    spread = jnp.repeat(cotangent.reshape(N_DP, block_rows, D), TOP, axis=1).astype(jnp.float32)
    routed = jnp.einsum("aiec,aid->eacd", weights, spread)
    return routed.reshape(EXPERTS, SLOTS, D).astype(jnp.bfloat16)


def one_expert(inputs):
    routed_e, weight_e, gate_e, up_e = inputs
    dact = jnp.dot(routed_e, weight_e.T, preferred_element_type=jnp.float32)
    gate_f = gate_e.astype(jnp.float32)
    up_f = up_e.astype(jnp.float32)
    sig = jax.nn.sigmoid(gate_f)
    silu_v = gate_f * sig
    grad_gate = (dact * up_f * sig * (1.0 + gate_f * (1.0 - sig))).astype(jnp.bfloat16)
    grad_up = (dact * silu_v).astype(jnp.bfloat16)
    act = (silu_v * up_f).astype(jnp.bfloat16)
    grad_down = jnp.dot(act.T, routed_e, preferred_element_type=jnp.float32).astype(jnp.bfloat16)
    return grad_gate, grad_up, grad_down


def reference(cotangent, expert_ids, route_probs, saved_gate, saved_up, down_weight):
    routed = routed_rows(cotangent, expert_ids, route_probs)
    weights = down_weight.reshape(EXPERTS, FF, D)
    gates = jnp.transpose(saved_gate.reshape(SLOTS, EXPERTS, FF), (1, 0, 2))
    ups = jnp.transpose(saved_up.reshape(SLOTS, EXPERTS, FF), (1, 0, 2))
    grad_gate, grad_up, grad_down = lax.map(one_expert, (routed, weights, gates, ups))
    grad_gate = jnp.transpose(grad_gate, (1, 0, 2)).reshape(SLOTS, EXPERTS * FF)
    grad_up = jnp.transpose(grad_up, (1, 0, 2)).reshape(SLOTS, EXPERTS * FF)
    return grad_gate, grad_up, grad_down.reshape(EXPERTS * FF, D)
```

```python
import jax
import jax.numpy as jnp
from jax import lax
from jax.experimental import pallas as pl
from jax.experimental.pallas import tpu as pltpu
from jax.sharding import PartitionSpec as P

D = 1536
HALF = D // 2
HID = 256
META = 128
MESH = pl.DeviceIdType.MESH
F32 = jnp.float32
BF16 = jnp.bfloat16


def kernel(
    cot_ref, ids_ref, probs_ref, gate_hbm, up_hbm, w_hbm,
    gg_ref, gu_ref, gd_ref,
    tok, tok32, block, rows, gate, up, w, f_gate, f_up, act_t, dact, other, gd_acc,
    load_sem, a_send, a_recv, b_send, b_recv, z_send, z_recv,
    s1_send, s1_recv, s1f_send, s1f_recv, s2_send, s2_recv, s2f_send, s2f_recv,
    t_send, t_recv,
):
    z, c, core = lax.axis_index("dp"), lax.axis_index("ctx"), lax.axis_index("tp")
    x, y = c // 4, c % 4
    grp, lane_z = z // 4, z % 4
    k, h = c // 2, c % 2
    mate = (k - grp + 8) % 8
    partner = mate * 4 + lane_z
    alone = mate == grp

    loads = [
        pltpu.make_async_copy(src, dst, load_sem.at[n])
        for n, (src, dst) in enumerate(((gate_hbm, gate), (up_hbm, up), (w_hbm, w)))
    ]
    for load in loads:
        load.start()

    barrier = pltpu.get_barrier_semaphore()
    for d in range(1, 16):
        pl.semaphore_signal(barrier, inc=1, device_id={"ctx": (c + d) % 16}, device_id_type=MESH)
    for d in range(1, 4):
        pl.semaphore_signal(barrier, inc=1, device_id={"dp": grp * 4 + (lane_z + d) % 4}, device_id_type=MESH)
    pl.semaphore_signal(barrier, inc=1, device_id={"tp": 1 - core}, device_id_type=MESH)

    @pl.when(jnp.logical_not(alone))
    def _():
        pl.semaphore_signal(barrier, inc=1, device_id={"dp": partner}, device_id_type=MESH)

    tok[c, :, :D] = cot_ref[...]
    flat = jnp.concatenate(
        [ids_ref[...].astype(F32), probs_ref[...].astype(F32), jnp.zeros((4, 4), F32)], axis=0
    )
    flat = jnp.concatenate([flat, jnp.zeros((8, META - 4), F32)], axis=1)
    side = jnp.transpose(flat)[:4, :]
    tok[c, :, D:] = jnp.concatenate([side, jnp.zeros((4, META - 8), F32)], axis=1).astype(BF16)

    pl.semaphore_wait(barrier, jnp.where(alone, 19, 20))

    def a_copy(d, whose, to):
        return pltpu.make_async_remote_copy(
            src_ref=tok.at[whose], dst_ref=tok.at[whose],
            send_sem=a_send.at[d - 1], recv_sem=a_recv.at[d - 1],
            device_id={"ctx": to}, device_id_type=MESH,
        )

    for d in range(1, 16):
        a_copy(d, c, (c + d) % 16).start()
    for d in range(1, 16):
        a_copy(d, (c + 16 - d) % 16, c).wait_recv()

    for n in range(16):
        tok32[4 * n:4 * n + 4, :] = tok[n].astype(F32)
    side = tok32[:, D:]
    expert = mate.astype(F32)
    hit0, hit1 = side[:, 0:1] == expert, side[:, 1:2] == expert
    weight = jnp.where(hit0, side[:, 2:3], jnp.where(hit1, side[:, 3:4], 0.0))
    hit = jnp.where(hit0 | hit1, 1.0, 0.0)
    before = (
        lax.broadcasted_iota(jnp.int32, (64, 64), 0) > lax.broadcasted_iota(jnp.int32, (64, 64), 1)
    )
    slot = jnp.dot(
        jnp.where(before, 1.0, 0.0).astype(BF16),
        jnp.broadcast_to(hit, (64, META)).astype(BF16),
        preferred_element_type=F32,
    )
    wanted = lax.broadcasted_iota(jnp.int32, (64, META), 1) + 16 * h
    place = jnp.where((slot == wanted.astype(F32)) & (jnp.broadcast_to(hit, (64, META)) > 0.5),
                      jnp.broadcast_to(weight, (64, META)), 0.0)
    place = jnp.transpose(place)[:16, :].astype(BF16)
    made = jnp.dot(place, tok32[:, :D].astype(BF16), preferred_element_type=F32).astype(BF16)

    def b_copy():
        return pltpu.make_async_remote_copy(
            src_ref=block, dst_ref=rows.at[grp, lane_z, h],
            send_sem=b_send, recv_sem=b_recv,
            device_id={"dp": partner}, device_id_type=MESH,
        )

    own = mate

    @pl.when(alone)
    def _():
        rows[own, lane_z, h] = made

    @pl.when(jnp.logical_not(alone))
    def _():
        block[...] = made
        copy = b_copy()
        copy.start()
        copy.wait_recv()

    def z_copy(d, whose, to):
        return pltpu.make_async_remote_copy(
            src_ref=rows.at[own, whose, h], dst_ref=rows.at[own, whose, h],
            send_sem=z_send.at[d - 1], recv_sem=z_recv.at[d - 1],
            device_id={"dp": grp * 4 + to}, device_id_type=MESH,
        )

    for d in range(1, 4):
        z_copy(d, lane_z, (lane_z + d) % 4).start()
    for d in range(1, 4):
        z_copy(d, (lane_z + 4 - d) % 4, lane_z).wait_recv()

    def where_of(half, p, q):
        xx, yy = (p, q) if half == 0 else (q, p)
        return (2 * xx + yy // 2 - grp + 8) % 8, yy % 2

    def ctx_of(half, p, q):
        xx, yy = (p, q) if half == 0 else (q, p)
        return xx * 4 + yy

    def near(v, step):
        return (v + 4 + step) % 4

    def piece(half, p, q, part):
        jj, hh = where_of(half, p, q)
        lanes = {None: pl.ds(0, 4), 0: pl.ds(0, 2), 1: pl.ds(2, 2)}[part]
        return rows.at[jj, lanes, hh, :, pl.ds(half * HALF, HALF)]

    def xy_copy(half, p, q, part, sems, to):
        ref = piece(half, p, q, part)
        return pltpu.make_async_remote_copy(
            src_ref=ref, dst_ref=ref, send_sem=sems[0], recv_sem=sems[1],
            device_id={"ctx": to}, device_id_type=MESH,
        )

    pos = ((x, y), (y, x))
    STEP = (1, -1)

    def s1(half, side, whose_p, to_p):
        p, q = pos[half]
        sems = (s1_send.at[half, side], s1_recv.at[half, side])
        return xy_copy(half, whose_p, q, None, sems, ctx_of(half, to_p, q))

    def s1f(half, side, whose_p, to_p):
        p, q = pos[half]
        sems = (s1f_send.at[half, side], s1f_recv.at[half, side])
        return xy_copy(half, whose_p, q, side, sems, ctx_of(half, to_p, q))

    ORDER = (0, -1, 1, 2)

    def s2(half, n, side, whose_q, to_q):
        p, q = pos[half]
        sems = (s2_send.at[half, n, side], s2_recv.at[half, n, side])
        return xy_copy(half, near(p, ORDER[n]), whose_q, None, sems, ctx_of(half, p, to_q))

    def s2f(half, n, side, whose_q, to_q):
        p, q = pos[half]
        sems = (s2f_send.at[half, n, side], s2f_recv.at[half, n, side])
        return xy_copy(half, near(p, ORDER[n]), whose_q, side, sems, ctx_of(half, p, to_q))

    def start_s2(half, n):
        q = pos[half][1]
        for side in (0, 1):
            s2(half, n, side, q, near(q, STEP[side])).start()

    def pass_s2(half, n):
        q = pos[half][1]
        for side in (0, 1):
            s2(half, n, side, near(q, -STEP[side]), q).wait_recv()
            s2f(half, n, side, near(q, -STEP[side]), near(q, STEP[side])).start()

    def end_s2(half, n):
        q = pos[half][1]
        for side in (0, 1):
            s2f(half, n, side, near(q, -2 * STEP[side]), q).wait_recv()

    for half in (0, 1):
        p = pos[half][0]
        for side in (0, 1):
            s1(half, side, p, near(p, STEP[side])).start()
    for half in (0, 1):
        start_s2(half, 0)
    for half in (0, 1):
        p = pos[half][0]
        for side in (0, 1):
            s1(half, side, near(p, -STEP[side]), p).wait_recv()
            s1f(half, side, near(p, -STEP[side]), near(p, STEP[side])).start()
    for half in (0, 1):
        start_s2(half, 1)
        start_s2(half, 2)
    for half in (0, 1):
        pass_s2(half, 0)
    for half in (0, 1):
        p = pos[half][0]
        for side in (0, 1):
            s1f(half, side, near(p, -2 * STEP[side]), p).wait_recv()
        start_s2(half, 3)

    for load in loads:
        load.wait()
    dact[...] = jnp.zeros_like(dact)
    gd_acc[...] = jnp.zeros_like(gd_acc)

    def factors(n, carry):
        g, u = gate[n].astype(F32), up[n].astype(F32)
        s = jax.nn.sigmoid(g)
        f_up[n] = g * s
        f_gate[n] = u * s * (1.0 + g * (1.0 - s))
        return carry

    lax.fori_loop(0, 8, factors, 0)

    def act_of(half, n):
        p = near(pos[half][0], ORDER[n])
        parts = []
        for q in range(4):
            jj, hh = where_of(half, p, q)
            parts.append((f_up[jj, :, hh] * up[jj, :, hh].astype(F32)).reshape(64, HID))
        return jnp.concatenate(parts, axis=0)

    for half in (0, 1):
        for n in range(4):
            act_t[half, n] = jnp.transpose(act_of(half, n)).astype(BF16)

    def use(half, n):
        p = near(pos[half][0], ORDER[n])
        cols = pl.ds(half * HALF, HALF)
        spots = [where_of(half, p, q) for q in range(4)]
        got = jnp.concatenate([rows[jj, :, hh, :, cols].reshape(64, HALF) for jj, hh in spots], axis=0)
        part = lax.dot_general(got, w[:, cols], (((1,), (1,)), ((), ())), preferred_element_type=F32)
        for q, (jj, hh) in enumerate(spots):
            dact[jj, :, hh] += part[64 * q:64 * q + 64].reshape(4, 16, HID)
        gd_acc[:, cols] += jnp.dot(act_t[half, n], got, preferred_element_type=F32)

    for n in (1, 2):
        for half in (0, 1):
            pass_s2(half, n)
    for half in (0, 1):
        end_s2(half, 0)
        use(half, 0)
    for half in (0, 1):
        pass_s2(half, 3)
    for n in (1, 2, 3):
        for half in (0, 1):
            end_s2(half, n)
            use(half, n)

    def t_copy(n):
        return pltpu.make_async_remote_copy(
            src_ref=dact.at[pl.ds(2 * n, 2)], dst_ref=other.at[pl.ds(2 * n, 2)],
            send_sem=t_send.at[n], recv_sem=t_recv.at[n],
            device_id={"tp": 1 - core}, device_id_type=MESH,
        )

    for n in range(4):
        t_copy(n).start()
    gd_ref[...] = gd_acc[...].astype(BF16)
    for n in range(4):
        t_copy(n).wait_recv()
        for m in (2 * n, 2 * n + 1):
            total = dact[m] + other[m]
            gg_ref[m] = (total * f_gate[m]).astype(BF16)
            gu_ref[m] = (total * f_up[m]).astype(BF16)

    for d in range(1, 16):
        a_copy(d, c, (c + d) % 16).wait_send()

    @pl.when(jnp.logical_not(alone))
    def _():
        b_copy().wait_send()

    for d in range(1, 4):
        z_copy(d, lane_z, (lane_z + d) % 4).wait_send()
    for half in (0, 1):
        p, q = pos[half]
        for side in (0, 1):
            s1(half, side, p, near(p, STEP[side])).wait_send()
            s1f(half, side, near(p, -STEP[side]), near(p, STEP[side])).wait_send()
            for n in range(4):
                s2(half, n, side, q, near(q, STEP[side])).wait_send()
                s2f(half, n, side, near(q, -STEP[side]), near(q, STEP[side])).wait_send()
    for n in range(4):
        t_copy(n).wait_send()


def body(cotangent, expert_ids, route_probs, saved_gate, saved_up, down_weight):
    shape5 = (8, 4, 2, 16, HID)
    vmem, hbm = pl.BlockSpec(memory_space=pltpu.VMEM), pl.BlockSpec(memory_space=pl.ANY)
    dma = pltpu.SemaphoreType.DMA
    gg, gu, gd = pl.pallas_call(
        kernel,
        out_shape=(
            jax.ShapeDtypeStruct(shape5, BF16),
            jax.ShapeDtypeStruct(shape5, BF16),
            jax.ShapeDtypeStruct((HID, D), BF16),
        ),
        in_specs=[vmem, vmem, vmem, hbm, hbm, hbm],
        out_specs=(vmem, vmem, vmem),
        scratch_shapes=[
            pltpu.VMEM((16, 4, D + META), BF16),
            pltpu.VMEM((64, D + META), F32),
            pltpu.VMEM((16, D), BF16),
            pltpu.VMEM((8, 4, 2, 16, D), BF16),
            pltpu.VMEM(shape5, BF16),
            pltpu.VMEM(shape5, BF16),
            pltpu.VMEM((HID, D), BF16),
            pltpu.VMEM(shape5, F32),
            pltpu.VMEM(shape5, F32),
            pltpu.VMEM((2, 4, HID, HID), BF16),
            pltpu.VMEM(shape5, F32),
            pltpu.VMEM(shape5, F32),
            pltpu.VMEM((HID, D), F32),
            dma((3,)), dma((15,)), dma((15,)), dma, dma, dma((3,)), dma((3,)),
            dma((2, 2)), dma((2, 2)), dma((2, 2)), dma((2, 2)),
            dma((2, 4, 2)), dma((2, 4, 2)), dma((2, 4, 2)), dma((2, 4, 2)),
            dma((4,)), dma((4,)),
        ],
        compiler_params=pltpu.CompilerParams(
            collective_id=0, has_side_effects=True, vmem_limit_bytes=60 * 1024 * 1024
        ),
    )(
        cotangent, expert_ids.T, route_probs.T,
        saved_gate.reshape(shape5), saved_up.reshape(shape5), down_weight,
    )
    return gg.reshape(1024, HID), gu.reshape(1024, HID), gd


def solution(mesh):
    return jax.shard_map(
        body,
        mesh=mesh,
        in_specs=(
            P(("dp", "ctx"), "tp"),
            P(("dp", "ctx"), None),
            P(("dp", "ctx"), None),
            P(None, ("dp", "ctx")),
            P(None, ("dp", "ctx")),
            P(("dp", "ctx"), "tp"),
        ),
        out_specs=(P(None, ("dp", "ctx")), P(None, ("dp", "ctx")), P(("dp", "ctx"), "tp")),
        check_vma=False,
    )
```

```python
import jax
import jax.numpy as jnp
from jax import lax
from jax.experimental import pallas as pl
from jax.experimental.pallas import tpu as pltpu
from jax.sharding import PartitionSpec as P

D = 1536
QUARTER = D // 4
HID = 256
META = 128
MESH = pl.DeviceIdType.MESH
F32 = jnp.float32
BF16 = jnp.bfloat16


def kernel(
    cot_hbm, ids_hbm, probs_hbm, gate_hbm, up_hbm, w_hbm,
    gg_ref, gu_ref, gd_ref,
    cot_ref, ids_ref, probs_ref, mine, tok, tok32, block, rows, gate, up, w, f_gate, f_up, act_t, dact, other, gd_acc,
    load_sem, a_send, a_recv, b_send, b_recv, z_send, z_recv,
    s1_send, s1_recv, s1f_send, s1f_recv, s2_send, s2_recv, s2f_send, s2f_recv,
    t_send, t_recv,
):
    z, c, core = lax.axis_index("dp"), lax.axis_index("ctx"), lax.axis_index("tp")
    x, y = c // 4, c % 4
    grp, lane_z = z // 4, z % 4
    mate = (y - grp + 8) % 4
    self_half = grp // 4
    alone = mate == grp % 4

    def to_other(s):
        return jnp.logical_not(alone & (self_half == s))

    first = [
        pltpu.make_async_copy(src, dst, load_sem.at[12 + n])
        for n, (src, dst) in enumerate(((cot_hbm, cot_ref), (ids_hbm, ids_ref), (probs_hbm, probs_ref)))
    ]
    for load in first:
        load.start()
    loads = []
    for src, dst in ((gate_hbm, gate), (up_hbm, up)):
        for r in range(4):
            loads.append((src.at[:, (lane_z + r) % 4], dst.at[:, r]))
    for m in range(4):
        loads.append((w_hbm.at[:, pl.ds(QUARTER * m, QUARTER)], w.at[m]))
    loads = [pltpu.make_async_copy(src, dst, load_sem.at[n]) for n, (src, dst) in enumerate(loads)]
    for load in loads:
        load.start()

    barrier = pltpu.get_barrier_semaphore()
    for s in range(2):
        @pl.when(to_other(s))
        def _():
            pl.semaphore_signal(
                barrier, inc=1, device_id={"dp": (mate + 4 * s) * 4 + lane_z}, device_id_type=MESH
            )
    for d in range(1, 16):
        pl.semaphore_signal(barrier, inc=1, device_id={"ctx": (c + d) % 16}, device_id_type=MESH)
    for d in range(1, 4):
        pl.semaphore_signal(barrier, inc=1, device_id={"dp": grp * 4 + (lane_z + d) % 4}, device_id_type=MESH)
    pl.semaphore_signal(barrier, inc=1, device_id={"tp": 1 - core}, device_id_type=MESH)

    for load in first:
        load.wait()
    flat = jnp.concatenate(
        [ids_ref[...].astype(F32), probs_ref[...].astype(F32), jnp.zeros((4, 4), F32)], axis=0
    )
    flat = jnp.concatenate([flat, jnp.zeros((8, META - 4), F32)], axis=1)
    side = jnp.transpose(flat)[:4, :]
    side = jnp.concatenate([side, jnp.zeros((4, META - 8), F32)], axis=1).astype(BF16)
    for q in range(4):
        mine[q, :, :QUARTER] = cot_ref[:, QUARTER * q:QUARTER * q + QUARTER]
        mine[q, :, QUARTER:] = side
    tok[c] = mine[x]

    pl.semaphore_wait(barrier, jnp.where(alone, 20, 21))

    def a_copy(d):
        to = (c + d) % 16
        return pltpu.make_async_remote_copy(
            src_ref=mine.at[to // 4], dst_ref=tok.at[c],
            send_sem=a_send.at[d - 1], recv_sem=a_recv.at[d - 1],
            device_id={"ctx": to}, device_id_type=MESH,
        )

    for d in range(1, 16):
        a_copy(d).start()

    def factors(n, carry):
        g, u = gate[n].reshape(128, HID).astype(F32), up[n].reshape(128, HID).astype(F32)
        s = jax.nn.sigmoid(g)
        silu = g * s
        f_up[n] = silu
        f_gate[n] = u * s * (1.0 + g * (1.0 - s))
        act_t[n] = jnp.transpose(silu * u).astype(BF16)
        return carry

    for load in loads:
        load.wait()
    lax.fori_loop(0, 4, factors, 0)

    for d in range(1, 16):
        a_copy(d).wait_recv()

    for n in range(16):
        tok32[4 * n:4 * n + 4, :] = tok[n].astype(F32)
    side = tok32[:, QUARTER:]
    lanes = lax.broadcasted_iota(jnp.int32, (64, META), 1)
    expert = (mate + 4 * (lanes // 32)).astype(F32)
    hit0, hit1 = side[:, 0:1] == expert, side[:, 1:2] == expert
    weight = jnp.where(hit0, side[:, 2:3], jnp.where(hit1, side[:, 3:4], 0.0))
    hit = jnp.where(hit0 | hit1, 1.0, 0.0)
    before = (
        lax.broadcasted_iota(jnp.int32, (64, 64), 0) > lax.broadcasted_iota(jnp.int32, (64, 64), 1)
    )
    slot = jnp.dot(
        jnp.where(before, 1.0, 0.0).astype(BF16), hit.astype(BF16), preferred_element_type=F32
    )
    place = jnp.where((slot == (lanes % 32).astype(F32)) & (hit > 0.5), weight, 0.0)
    place = jnp.transpose(place)[:64, :].astype(BF16)
    made = jnp.dot(place, tok32[:, :QUARTER].astype(BF16), preferred_element_type=F32).astype(BF16)
    block[...] = made.reshape(2, 2, 16, QUARTER)

    def b_copy(s, arrives):
        return pltpu.make_async_remote_copy(
            src_ref=block.at[s], dst_ref=rows.at[x, grp, 0],
            send_sem=b_send.at[s], recv_sem=b_recv.at[arrives],
            device_id={"dp": (mate + 4 * s) * 4 + lane_z}, device_id_type=MESH,
        )

    for s in range(2):
        @pl.when(to_other(s))
        def _():
            b_copy(s, self_half).start()

    for s in range(2):
        @pl.when(jnp.logical_not(to_other(s)))
        def _():
            rows[x, grp, 0] = block[s]

    def z_copy(s, d):
        return pltpu.make_async_remote_copy(
            src_ref=rows.at[x, mate + 4 * s, 0], dst_ref=rows.at[x, mate + 4 * s, 4 - d],
            send_sem=z_send.at[s, d - 1], recv_sem=z_recv.at[s, d - 1],
            device_id={"dp": grp * 4 + (lane_z + d) % 4}, device_id_type=MESH,
        )

    lax.fori_loop(4, 8, factors, 0)
    gd_acc[...] = jnp.zeros_like(gd_acc)

    pos = ((x, y), (y, x))
    STEP = (1, -1)
    ORDER = (0, -1, 1, 2)
    BOTH = (0, 1)

    def near(v, step):
        return (v + 4 + step) % 4

    def xy_copy(t, half, p, q, part, sems, to_p, to_q):
        xx, yy = (p, q) if half == 0 else (q, p)
        to_x, to_y = (to_p, to_q) if half == 0 else (to_q, to_p)
        cut = {None: pl.ds(0, 2), 0: pl.ds(0, 1), 1: pl.ds(1, 1)}[part]
        ref = rows.at[xx, (yy - grp + 8) % 4 + 4 * half, (pl.ds(0, 1), pl.ds(1, 3))[t], cut]
        return pltpu.make_async_remote_copy(
            src_ref=ref, dst_ref=ref, send_sem=sems[0], recv_sem=sems[1],
            device_id={"ctx": to_x * 4 + to_y}, device_id_type=MESH,
        )

    def s1(t, half, side, whose, to):
        q = pos[half][1]
        sems = (s1_send.at[t, half, side], s1_recv.at[t, half, side])
        return xy_copy(t, half, whose, q, None, sems, to, q)

    def s1f(t, half, side, whose, to):
        q = pos[half][1]
        sems = (s1f_send.at[t, half, side], s1f_recv.at[t, half, side])
        return xy_copy(t, half, whose, q, side, sems, to, q)

    def s2(t, half, n, side, whose, to):
        p = pos[half][0]
        sems = (s2_send.at[t, half, n, side], s2_recv.at[t, half, n, side])
        return xy_copy(t, half, near(p, ORDER[n]), whose, None, sems, p, to)

    def s2f(t, half, n, side, whose, to):
        p = pos[half][0]
        sems = (s2f_send.at[t, half, n, side], s2f_recv.at[t, half, n, side])
        return xy_copy(t, half, near(p, ORDER[n]), whose, side, sems, p, to)

    def start_s1(t):
        for side in BOTH:
            for half in BOTH:
                p = pos[half][0]
                s1(t, half, side, p, near(p, STEP[side])).start()

    def start_s2(t, n):
        for side in BOTH:
            for half in BOTH:
                q = pos[half][1]
                s2(t, half, n, side, q, near(q, STEP[side])).start()

    def pass_s1(t):
        for side in BOTH:
            for half in BOTH:
                p = pos[half][0]
                s1(t, half, side, near(p, -STEP[side]), p).wait_recv()
                s1f(t, half, side, near(p, -STEP[side]), near(p, STEP[side])).start()
        start_s2(t, 1)
        start_s2(t, 2)

    def end_s1(t):
        for half in BOTH:
            p = pos[half][0]
            for side in BOTH:
                s1f(t, half, side, near(p, -2 * STEP[side]), p).wait_recv()
        start_s2(t, 3)

    def pass_s2(t, n):
        for side in BOTH:
            for half in BOTH:
                q = pos[half][1]
                s2(t, half, n, side, near(q, -STEP[side]), q).wait_recv()
                s2f(t, half, n, side, near(q, -STEP[side]), near(q, STEP[side])).start()

    def end_s2(half, n):
        q = pos[half][1]
        for t in BOTH:
            for side in BOTH:
                s2f(t, half, n, side, near(q, -2 * STEP[side]), q).wait_recv()

    def t_copy(n):
        slab = dact.at[n]
        return pltpu.make_async_remote_copy(
            src_ref=slab, dst_ref=other.at[n],
            send_sem=t_send.at[n], recv_sem=t_recv.at[n],
            device_id={"tp": 1 - core}, device_id_type=MESH,
        )

    def use0(n):
        q = near(x, ORDER[n])
        got = rows[q, 0:4].reshape(512, QUARTER)
        part = lax.dot_general(got, w[q], (((1,), (1,)), ((), ())), preferred_element_type=F32)
        part = part.reshape(4, 128, HID)
        dact[0:4] = part if n == 0 else dact[0:4] + part
        total = gd_acc[q]
        for m in range(4):
            total += jnp.dot(act_t[m], got[128 * m:128 * m + 128], preferred_element_type=F32)
        gd_acc[q] = total

    def use1(n):
        m = (near(y, ORDER[n]) - grp + 8) % 4 + 4
        total = jnp.zeros((128, HID), F32)
        for q in range(4):
            got = rows[q, m].reshape(128, QUARTER)
            total += lax.dot_general(got, w[q], (((1,), (1,)), ((), ())), preferred_element_type=F32)
            gd_acc[q] += jnp.dot(act_t[m], got, preferred_element_type=F32)
        dact[m] = total
        t_copy(m).start()

    def finish(m):
        t_copy(m).wait_recv()
        total = dact[m] + other[m]
        for ref, factor in ((gg_ref, f_gate), (gu_ref, f_up)):
            value = (total * factor[m]).astype(BF16)
            for r in range(4):
                ref[m, (lane_z + r) % 4] = value[32 * r:32 * r + 32]

    def block_of(n):
        return (near(y, ORDER[n]) - grp + 8) % 4 + 4

    for s in BOTH:
        @pl.when(to_other(s))
        def _():
            b_copy(s, s).wait_recv()
        for d in range(1, 4):
            z_copy(s, d).start()
    start_s1(0)
    start_s2(0, 0)
    pass_s1(0)
    pass_s2(0, 0)
    for s in BOTH:
        for d in range(1, 4):
            z_copy(s, d).wait_recv()
    start_s1(1)
    start_s2(1, 0)
    end_s1(0)
    pass_s2(0, 1)
    pass_s2(0, 2)
    pass_s1(1)
    pass_s2(0, 3)
    pass_s2(1, 0)
    end_s1(1)
    pass_s2(1, 1)
    pass_s2(1, 2)
    for half in BOTH:
        end_s2(half, 0)
    use1(0)
    use0(0)
    pass_s2(1, 3)
    for n in (1, 2):
        end_s2(1, n)
        use1(n)
        end_s2(0, n)
        use0(n)
    for n in (0, 1):
        finish(block_of(n))
    end_s2(0, 3)
    use0(3)
    for m in range(4):
        t_copy(m).start()
    end_s2(1, 3)
    use1(3)

    for q in range(4):
        gd_ref[:, QUARTER * q:QUARTER * q + QUARTER] = gd_acc[q].astype(BF16)
    finish(block_of(2))
    for m in range(4):
        finish(m)
    finish(block_of(3))

    for d in range(1, 16):
        a_copy(d).wait_send()
    for s in BOTH:
        @pl.when(to_other(s))
        def _():
            b_copy(s, self_half).wait_send()
        for d in range(1, 4):
            z_copy(s, d).wait_send()
    for t in BOTH:
        for half in BOTH:
            p, q = pos[half]
            for side in BOTH:
                s1(t, half, side, p, near(p, STEP[side])).wait_send()
                s1f(t, half, side, near(p, -STEP[side]), near(p, STEP[side])).wait_send()
                for n in range(4):
                    s2(t, half, n, side, q, near(q, STEP[side])).wait_send()
                    s2f(t, half, n, side, near(q, -STEP[side]), near(q, STEP[side])).wait_send()
    for n in range(8):
        t_copy(n).wait_send()


def write_out(gg_ref, gu_ref, gd_ref, gg_out, gu_out, gd_out, sem):
    copies = []
    for src, dst, amount in ((gg_ref, gg_out, 256), (gu_ref, gu_out, 256), (gd_ref, gd_out, 64)):
        for m in range(4):
            cut = pl.ds(m * amount, amount)
            copies.append(pltpu.make_async_copy(src.at[cut], dst.at[cut], sem.at[len(copies)]))
    for copy in copies:
        copy.start()
    for copy in copies:
        copy.wait()


def body(cotangent, expert_ids, route_probs, saved_gate, saved_up, down_weight):
    slabs, parts = (8, 128, HID), (8, 4, 32, HID)
    vmem, hbm, any_ = (pl.BlockSpec(memory_space=m) for m in (pltpu.VMEM, pltpu.HBM, pl.ANY))
    dma = pltpu.SemaphoreType.DMA
    gg, gu, gd = pl.pallas_call(
        kernel,
        out_shape=(
            jax.ShapeDtypeStruct(parts, BF16),
            jax.ShapeDtypeStruct(parts, BF16),
            jax.ShapeDtypeStruct((HID, D), BF16),
        ),
        in_specs=[hbm] * 6,
        out_specs=(vmem, vmem, vmem),
        scratch_shapes=[
            pltpu.VMEM((4, D), BF16),
            pltpu.VMEM((2, 4), jnp.int32),
            pltpu.VMEM((2, 4), BF16),
            pltpu.VMEM((4, 4, QUARTER + META), BF16),
            pltpu.VMEM((16, 4, QUARTER + META), BF16),
            pltpu.VMEM((64, QUARTER + META), F32),
            pltpu.VMEM((2, 2, 16, QUARTER), BF16),
            pltpu.VMEM((4, 8, 4, 2, 16, QUARTER), BF16),
            pltpu.VMEM(parts, BF16),
            pltpu.VMEM(parts, BF16),
            pltpu.VMEM((4, HID, QUARTER), BF16),
            pltpu.VMEM(slabs, F32),
            pltpu.VMEM(slabs, F32),
            pltpu.VMEM((8, HID, 128), BF16),
            pltpu.VMEM(slabs, F32),
            pltpu.VMEM(slabs, F32),
            pltpu.VMEM((4, HID, QUARTER), F32),
            dma((15,)), dma((15,)), dma((15,)), dma((2,)), dma((2,)), dma((2, 3)), dma((2, 3)),
            dma((2, 2, 2)), dma((2, 2, 2)), dma((2, 2, 2)), dma((2, 2, 2)),
            dma((2, 2, 4, 2)), dma((2, 2, 4, 2)), dma((2, 2, 4, 2)), dma((2, 2, 4, 2)),
            dma((8,)), dma((8,)),
        ],
        compiler_params=pltpu.CompilerParams(
            collective_id=0, has_side_effects=True, vmem_limit_bytes=40 * 1024 * 1024
        ),
    )(
        *(
            pltpu.with_memory_space_constraint(a, pltpu.HBM)
            for a in (
                cotangent, expert_ids.T, route_probs.T,
                saved_gate.reshape(parts), saved_up.reshape(parts), down_weight,
            )
        ),
    )
    return pl.pallas_call(
        write_out,
        out_shape=(
            jax.ShapeDtypeStruct((1024, HID), BF16),
            jax.ShapeDtypeStruct((1024, HID), BF16),
            jax.ShapeDtypeStruct((HID, D), BF16),
        ),
        in_specs=[vmem] * 3,
        out_specs=(any_,) * 3,
        scratch_shapes=[dma((12,))],
        compiler_params=pltpu.CompilerParams(vmem_limit_bytes=4 * 1024 * 1024),
    )(gg.reshape(1024, HID), gu.reshape(1024, HID), gd)


def solution(mesh):
    return jax.shard_map(
        body,
        mesh=mesh,
        in_specs=(
            P(("dp", "ctx"), "tp"),
            P(("dp", "ctx"), None),
            P(("dp", "ctx"), None),
            P(None, ("dp", "ctx")),
            P(None, ("dp", "ctx")),
            P(("dp", "ctx"), "tp"),
        ),
        out_specs=(P(None, ("dp", "ctx")), P(None, ("dp", "ctx")), P(("dp", "ctx"), "tp")),
        check_vma=False,
    )
```

```python
import jax
import jax.numpy as jnp
from jax import lax
from jax.experimental import pallas as pl
from jax.experimental.pallas import tpu as pltpu
from jax.sharding import PartitionSpec as P

D = 1536
QUARTER = D // 4
HID = 256
META = 128
MESH = pl.DeviceIdType.MESH
F32 = jnp.float32
BF16 = jnp.bfloat16


def kernel(
    cot_hbm, ids_hbm, probs_hbm, gate_hbm, up_hbm, w_hbm,
    gg_ref, gu_ref, gd_ref,
    cot_ref, ids_ref, probs_ref, mine, tok, tok32, block, rows, gate, up, w, f_gate, f_up, act_t, dact, other, gd_acc,
    load_sem, vouched, a_send, a_recv, b_send, b_recv, z_send, z_recv,
    s1_send, s1_recv, s1f_send, s1f_recv, s2_send, s2_recv, s2f_send, s2f_recv,
    t_send, t_recv,
):
    z, c, core = lax.axis_index("dp"), lax.axis_index("ctx"), lax.axis_index("tp")
    x, y = c // 4, c % 4
    grp, lane_z = z // 4, z % 4
    mate = (y - grp + 8) % 4
    self_half = grp // 4
    alone = mate == grp % 4

    def to_other(s):
        return jnp.logical_not(alone & (self_half == s))

    first = [
        pltpu.make_async_copy(src, dst, load_sem.at[12 + n])
        for n, (src, dst) in enumerate(((cot_hbm, cot_ref), (ids_hbm, ids_ref), (probs_hbm, probs_ref)))
    ]
    for load in first:
        load.start()
    loads = []
    for src, dst in ((gate_hbm, gate), (up_hbm, up)):
        for r in range(4):
            loads.append((src.at[:, (lane_z + r) % 4], dst.at[:, r]))
    for m in range(4):
        loads.append((w_hbm.at[:, pl.ds(QUARTER * m, QUARTER)], w.at[m]))
    loads = [pltpu.make_async_copy(src, dst, load_sem.at[n]) for n, (src, dst) in enumerate(loads)]
    for load in loads:
        load.start()

    barrier = pltpu.get_barrier_semaphore()
    turn = (y - 2 * grp + 16) % 4
    even = turn % 2 == 0

    def plane(off):
        return {"dp": (grp + off + 8) % 8 * 4 + lane_z}

    def greet(off):
        pl.semaphore_signal(barrier, inc=1, device_id=plane(off), device_id_type=MESH)

    @pl.when(even)
    def _():
        greet(2)
        greet(-2)

    @pl.when(jnp.logical_not(even))
    def _():
        greet(turn - 3 + (turn - 1) // 2 * 2)
        greet(1)
        greet(-1)

    for d in range(1, 16):
        pl.semaphore_signal(barrier, inc=1, device_id={"ctx": (c + d) % 16}, device_id_type=MESH)
    for d in range(1, 4):
        pl.semaphore_signal(barrier, inc=1, device_id={"dp": grp * 4 + (lane_z + d) % 4}, device_id_type=MESH)
    pl.semaphore_signal(barrier, inc=1, device_id={"tp": 1 - core}, device_id_type=MESH)

    for load in first:
        load.wait()
    flat = jnp.concatenate(
        [ids_ref[...].astype(F32), probs_ref[...].astype(F32), jnp.zeros((4, 4), F32)], axis=0
    )
    flat = jnp.concatenate([flat, jnp.zeros((8, META - 4), F32)], axis=1)
    side = jnp.transpose(flat)[:4, :]
    side = jnp.concatenate([side, jnp.zeros((4, META - 8), F32)], axis=1).astype(BF16)
    for q in range(4):
        mine[q, :, :QUARTER] = cot_ref[:, QUARTER * q:QUARTER * q + QUARTER]
        mine[q, :, QUARTER:] = side
    tok[c] = mine[x]

    pl.semaphore_wait(barrier, jnp.where(even, 21, 22))

    @pl.when(turn != 2)
    def _():
        target = jnp.where(turn == 0, -2, turn - 2)
        pl.semaphore_signal(vouched, inc=1, device_id=plane(target), device_id_type=MESH)

    def a_copy(d):
        to_x, to_y = (x + d // 4) % 4, (y + d % 4) % 4
        return pltpu.make_async_remote_copy(
            src_ref=mine.at[to_x], dst_ref=tok.at[c],
            send_sem=a_send.at[d - 1], recv_sem=a_recv.at[d - 1],
            device_id={"ctx": to_x * 4 + to_y}, device_id_type=MESH,
        )

    for d in (10, 6, 14, 9, 11, 2, 8, 5, 7, 13, 15, 1, 3, 4, 12):
        a_copy(d).start()

    def factors(n, carry):
        g, u = gate[n].reshape(128, HID).astype(F32), up[n].reshape(128, HID).astype(F32)
        s = jax.nn.sigmoid(g)
        silu = g * s
        f_up[n] = silu
        f_gate[n] = u * s * (1.0 + g * (1.0 - s))
        act_t[n] = jnp.transpose(silu * u).astype(BF16)
        return carry

    for load in loads:
        load.wait()
    lax.fori_loop(0, 4, factors, 0)

    for d in range(1, 16):
        a_copy(d).wait_recv()

    for n in range(16):
        tok32[4 * n:4 * n + 4, :] = tok[n].astype(F32)
    side = tok32[:, QUARTER:]
    lanes = lax.broadcasted_iota(jnp.int32, (64, META), 1)
    expert = (mate + 4 * (lanes // 32)).astype(F32)
    hit0, hit1 = side[:, 0:1] == expert, side[:, 1:2] == expert
    weight = jnp.where(hit0, side[:, 2:3], jnp.where(hit1, side[:, 3:4], 0.0))
    hit = jnp.where(hit0 | hit1, 1.0, 0.0)
    before = (
        lax.broadcasted_iota(jnp.int32, (64, 64), 0) > lax.broadcasted_iota(jnp.int32, (64, 64), 1)
    )
    slot = jnp.dot(
        jnp.where(before, 1.0, 0.0).astype(BF16), hit.astype(BF16), preferred_element_type=F32
    )
    place = jnp.where((slot == (lanes % 32).astype(F32)) & (hit > 0.5), weight, 0.0)
    place = jnp.transpose(place)[:64, :].astype(BF16)
    made = jnp.dot(place, tok32[:, :QUARTER].astype(BF16), preferred_element_type=F32).astype(BF16)
    block[...] = made.reshape(2, 2, 16, QUARTER)

    def b_copy(s, arrives):
        return pltpu.make_async_remote_copy(
            src_ref=block.at[s], dst_ref=rows.at[x, grp, 0],
            send_sem=b_send.at[s], recv_sem=b_recv.at[arrives],
            device_id={"dp": (mate + 4 * s) * 4 + lane_z}, device_id_type=MESH,
        )

    def far(s):
        off = (mate + 4 * s - grp + 8) % 8
        return (off >= 3) & (off <= 5)

    for s in range(2):
        @pl.when(to_other(s) & jnp.logical_not(far(s)))
        def _():
            b_copy(s, self_half).start()

    @pl.when(turn != 2)
    def _():
        pl.semaphore_wait(vouched, 1)

    for s in range(2):
        @pl.when(far(s))
        def _():
            b_copy(s, self_half).start()

    for s in range(2):
        @pl.when(jnp.logical_not(to_other(s)))
        def _():
            rows[x, grp, 0] = block[s]

    def z_copy(s, d):
        return pltpu.make_async_remote_copy(
            src_ref=rows.at[x, mate + 4 * s, 0], dst_ref=rows.at[x, mate + 4 * s, 4 - d],
            send_sem=z_send.at[s, d - 1], recv_sem=z_recv.at[s, d - 1],
            device_id={"dp": grp * 4 + (lane_z + d) % 4}, device_id_type=MESH,
        )

    lax.fori_loop(4, 8, factors, 0)
    gd_acc[...] = jnp.zeros_like(gd_acc)
    for d in range(1, 16):
        a_copy(d).wait_send()

    pos = ((x, y), (y, x))
    STEP = (1, -1)
    ORDER = (0, -1, 1, 2)
    BOTH = (0, 1)

    def near(v, step):
        return (v + 4 + step) % 4

    def xy_copy(t, half, p, q, part, sems, to_p, to_q):
        xx, yy = (p, q) if half == 0 else (q, p)
        to_x, to_y = (to_p, to_q) if half == 0 else (to_q, to_p)
        cut = {None: pl.ds(0, 2), 0: pl.ds(0, 1), 1: pl.ds(1, 1)}[part]
        ref = rows.at[xx, (yy - grp + 8) % 4 + 4 * half, (pl.ds(0, 1), pl.ds(1, 3))[t], cut]
        return pltpu.make_async_remote_copy(
            src_ref=ref, dst_ref=ref, send_sem=sems[0], recv_sem=sems[1],
            device_id={"ctx": to_x * 4 + to_y}, device_id_type=MESH,
        )

    def s1(t, half, side, whose, to):
        q = pos[half][1]
        sems = (s1_send.at[t, half, side], s1_recv.at[t, half, side])
        return xy_copy(t, half, whose, q, None, sems, to, q)

    def s1f(t, half, side, whose, to):
        q = pos[half][1]
        sems = (s1f_send.at[t, half, side], s1f_recv.at[t, half, side])
        return xy_copy(t, half, whose, q, side, sems, to, q)

    def s2(t, half, n, side, whose, to):
        p = pos[half][0]
        sems = (s2_send.at[t, half, n, side], s2_recv.at[t, half, n, side])
        return xy_copy(t, half, near(p, ORDER[n]), whose, None, sems, p, to)

    def s2f(t, half, n, side, whose, to):
        p = pos[half][0]
        sems = (s2f_send.at[t, half, n, side], s2f_recv.at[t, half, n, side])
        return xy_copy(t, half, near(p, ORDER[n]), whose, side, sems, p, to)

    def start_s1(t):
        for side in BOTH:
            for half in BOTH:
                p = pos[half][0]
                s1(t, half, side, p, near(p, STEP[side])).start()

    def start_s2(t, n):
        for side in BOTH:
            for half in BOTH:
                q = pos[half][1]
                s2(t, half, n, side, q, near(q, STEP[side])).start()

    def pass_s1(t):
        for side in BOTH:
            for half in BOTH:
                p = pos[half][0]
                s1(t, half, side, near(p, -STEP[side]), p).wait_recv()
                s1f(t, half, side, near(p, -STEP[side]), near(p, STEP[side])).start()
        start_s2(t, 1)
        start_s2(t, 2)

    def end_s1(t):
        for half in BOTH:
            p = pos[half][0]
            for side in BOTH:
                s1f(t, half, side, near(p, -2 * STEP[side]), p).wait_recv()
        start_s2(t, 3)

    def pass_s2(t, n):
        for side in BOTH:
            for half in BOTH:
                q = pos[half][1]
                s2(t, half, n, side, near(q, -STEP[side]), q).wait_recv()
                s2f(t, half, n, side, near(q, -STEP[side]), near(q, STEP[side])).start()

    def end_s2(half, n):
        q = pos[half][1]
        for t in BOTH:
            for side in BOTH:
                s2f(t, half, n, side, near(q, -2 * STEP[side]), q).wait_recv()

    def t_copy(n):
        slab = dact.at[n]
        return pltpu.make_async_remote_copy(
            src_ref=slab, dst_ref=other.at[n],
            send_sem=t_send.at[n], recv_sem=t_recv.at[n],
            device_id={"tp": 1 - core}, device_id_type=MESH,
        )

    def use0(n):
        q = near(x, ORDER[n])
        got = rows[q, 0:4].reshape(512, QUARTER)
        part = lax.dot_general(got, w[q], (((1,), (1,)), ((), ())), preferred_element_type=F32)
        part = part.reshape(4, 128, HID)
        dact[0:4] = part if n == 0 else dact[0:4] + part
        total = gd_acc[q]
        for m in range(4):
            total += jnp.dot(act_t[m], got[128 * m:128 * m + 128], preferred_element_type=F32)
        gd_acc[q] = total

    def use1(n):
        m = (near(y, ORDER[n]) - grp + 8) % 4 + 4
        total = jnp.zeros((128, HID), F32)
        for q in range(4):
            got = rows[q, m].reshape(128, QUARTER)
            total += lax.dot_general(got, w[q], (((1,), (1,)), ((), ())), preferred_element_type=F32)
            gd_acc[q] += jnp.dot(act_t[m], got, preferred_element_type=F32)
        dact[m] = total
        t_copy(m).start()

    def finish(m):
        t_copy(m).wait_recv()
        total = dact[m] + other[m]
        for ref, factor in ((gg_ref, f_gate), (gu_ref, f_up)):
            value = (total * factor[m]).astype(BF16)
            for r in range(4):
                ref[m, (lane_z + r) % 4] = value[32 * r:32 * r + 32]

    def block_of(n):
        return (near(y, ORDER[n]) - grp + 8) % 4 + 4

    for s in BOTH:
        @pl.when(to_other(s))
        def _():
            b_copy(s, s).wait_recv()
        for d in range(1, 4):
            z_copy(s, d).start()
    start_s1(0)
    start_s2(0, 0)
    pass_s1(0)
    pass_s2(0, 0)
    for s in BOTH:
        for d in range(1, 4):
            z_copy(s, d).wait_recv()
    start_s1(1)
    start_s2(1, 0)
    end_s1(0)
    pass_s2(0, 1)
    pass_s2(0, 2)
    pass_s1(1)
    pass_s2(0, 3)
    pass_s2(1, 0)
    end_s1(1)
    pass_s2(1, 1)
    pass_s2(1, 2)
    for half in BOTH:
        end_s2(half, 0)
    use1(0)
    use0(0)
    pass_s2(1, 3)
    for n in (1, 2):
        end_s2(1, n)
        use1(n)
        end_s2(0, n)
        use0(n)
    for n in (0, 1):
        finish(block_of(n))
    end_s2(0, 3)
    use0(3)
    for m in range(4):
        t_copy(m).start()
    end_s2(1, 3)
    use1(3)

    for q in range(4):
        gd_ref[:, QUARTER * q:QUARTER * q + QUARTER] = gd_acc[q].astype(BF16)
    finish(block_of(2))

    for s in BOTH:
        @pl.when(to_other(s))
        def _():
            b_copy(s, self_half).wait_send()
        for d in range(1, 4):
            z_copy(s, d).wait_send()
    for t in BOTH:
        for half in BOTH:
            p, q = pos[half]
            for side in BOTH:
                s1(t, half, side, p, near(p, STEP[side])).wait_send()
                s1f(t, half, side, near(p, -STEP[side]), near(p, STEP[side])).wait_send()
                for n in range(4):
                    s2(t, half, n, side, q, near(q, STEP[side])).wait_send()
                    s2f(t, half, n, side, near(q, -STEP[side]), near(q, STEP[side])).wait_send()
    for m in range(4):
        finish(m)
    finish(block_of(3))
    for n in range(8):
        t_copy(n).wait_send()


def write_out(gg_ref, gu_ref, gd_ref, gg_out, gu_out, gd_out, sem):
    copies = []
    for src, dst, amount in ((gg_ref, gg_out, 256), (gu_ref, gu_out, 256), (gd_ref, gd_out, 64)):
        for m in range(4):
            cut = pl.ds(m * amount, amount)
            copies.append(pltpu.make_async_copy(src.at[cut], dst.at[cut], sem.at[len(copies)]))
    for copy in copies:
        copy.start()
    for copy in copies:
        copy.wait()


def body(cotangent, expert_ids, route_probs, saved_gate, saved_up, down_weight):
    slabs, parts = (8, 128, HID), (8, 4, 32, HID)
    vmem, hbm, any_ = (pl.BlockSpec(memory_space=m) for m in (pltpu.VMEM, pltpu.HBM, pl.ANY))
    dma = pltpu.SemaphoreType.DMA
    gg, gu, gd = pl.pallas_call(
        kernel,
        out_shape=(
            jax.ShapeDtypeStruct(parts, BF16),
            jax.ShapeDtypeStruct(parts, BF16),
            jax.ShapeDtypeStruct((HID, D), BF16),
        ),
        in_specs=[hbm] * 6,
        out_specs=(vmem, vmem, vmem),
        scratch_shapes=[
            pltpu.VMEM((4, D), BF16),
            pltpu.VMEM((2, 4), jnp.int32),
            pltpu.VMEM((2, 4), BF16),
            pltpu.VMEM((4, 4, QUARTER + META), BF16),
            pltpu.VMEM((16, 4, QUARTER + META), BF16),
            pltpu.VMEM((64, QUARTER + META), F32),
            pltpu.VMEM((2, 2, 16, QUARTER), BF16),
            pltpu.VMEM((4, 8, 4, 2, 16, QUARTER), BF16),
            pltpu.VMEM(parts, BF16),
            pltpu.VMEM(parts, BF16),
            pltpu.VMEM((4, HID, QUARTER), BF16),
            pltpu.VMEM(slabs, F32),
            pltpu.VMEM(slabs, F32),
            pltpu.VMEM((8, HID, 128), BF16),
            pltpu.VMEM(slabs, F32),
            pltpu.VMEM(slabs, F32),
            pltpu.VMEM((4, HID, QUARTER), F32),
            dma((15,)), pltpu.SemaphoreType.REGULAR, dma((15,)), dma((15,)), dma((2,)), dma((2,)), dma((2, 3)), dma((2, 3)),
            dma((2, 2, 2)), dma((2, 2, 2)), dma((2, 2, 2)), dma((2, 2, 2)),
            dma((2, 2, 4, 2)), dma((2, 2, 4, 2)), dma((2, 2, 4, 2)), dma((2, 2, 4, 2)),
            dma((8,)), dma((8,)),
        ],
        compiler_params=pltpu.CompilerParams(
            collective_id=0, has_side_effects=True, vmem_limit_bytes=40 * 1024 * 1024
        ),
    )(
        *(
            pltpu.with_memory_space_constraint(a, pltpu.HBM)
            for a in (
                cotangent, expert_ids.T, route_probs.T,
                saved_gate.reshape(parts), saved_up.reshape(parts), down_weight,
            )
        ),
    )
    return pl.pallas_call(
        write_out,
        out_shape=(
            jax.ShapeDtypeStruct((1024, HID), BF16),
            jax.ShapeDtypeStruct((1024, HID), BF16),
            jax.ShapeDtypeStruct((HID, D), BF16),
        ),
        in_specs=[vmem] * 3,
        out_specs=(any_,) * 3,
        scratch_shapes=[dma((12,))],
        compiler_params=pltpu.CompilerParams(vmem_limit_bytes=4 * 1024 * 1024),
    )(gg.reshape(1024, HID), gu.reshape(1024, HID), gd)


def solution(mesh):
    return jax.shard_map(
        body,
        mesh=mesh,
        in_specs=(
            P(("dp", "ctx"), "tp"),
            P(("dp", "ctx"), None),
            P(("dp", "ctx"), None),
            P(None, ("dp", "ctx")),
            P(None, ("dp", "ctx")),
            P(("dp", "ctx"), "tp"),
        ),
        out_specs=(P(None, ("dp", "ctx")), P(None, ("dp", "ctx")), P(("dp", "ctx"), "tp")),
        check_vma=False,
    )
```

```python
import jax
import jax.numpy as jnp
from jax import lax
from jax.experimental import pallas as pl
from jax.experimental.pallas import tpu as pltpu
from jax.sharding import PartitionSpec as P

D = 1536
QUARTER = D // 4
HID = 256
META = 128
MESH = pl.DeviceIdType.MESH
F32 = jnp.float32
BF16 = jnp.bfloat16


def kernel(
    cot_hbm, ids_hbm, probs_hbm, gate_hbm, up_hbm, w_hbm,
    gg_ref, gu_ref, gd_ref,
    cot_ref, ids_ref, probs_ref, mine, tok, tok32, block, rows, gate, up, w, f_gate, f_up, act_t, dact, other, gd_acc,
    load_sem, vouched, a_send, a_recv, b_send, b_recv, z_send, z_recv,
    s1_send, s1_recv, s1f_send, s1f_recv, s2_send, s2_recv, s2f_send, s2f_recv,
    t_send, t_recv,
):
    z, c, core = lax.axis_index("dp"), lax.axis_index("ctx"), lax.axis_index("tp")
    x, y = c // 4, c % 4
    grp, lane_z = z // 4, z % 4
    mate = (y - grp + 8) % 4
    self_half = grp // 4
    alone = mate == grp % 4

    def to_other(s):
        return jnp.logical_not(alone & (self_half == s))

    first = [
        pltpu.make_async_copy(src, dst, load_sem.at[12 + n])
        for n, (src, dst) in enumerate(((cot_hbm, cot_ref), (ids_hbm, ids_ref), (probs_hbm, probs_ref)))
    ]
    for load in first:
        load.start()
    loads = []
    for src, dst in ((gate_hbm, gate), (up_hbm, up)):
        for r in range(4):
            loads.append((src.at[:, (lane_z + r) % 4], dst.at[:, r]))
    for m in range(4):
        loads.append((w_hbm.at[:, pl.ds(QUARTER * m, QUARTER)], w.at[m]))
    loads = [pltpu.make_async_copy(src, dst, load_sem.at[n]) for n, (src, dst) in enumerate(loads)]
    for load in loads:
        load.start()

    barrier = pltpu.get_barrier_semaphore()
    turn = (y - 2 * grp + 16) % 4
    even = turn % 2 == 0

    def plane(off):
        return {"dp": (grp + off + 8) % 8 * 4 + lane_z}

    def greet(off):
        pl.semaphore_signal(barrier, inc=1, device_id=plane(off), device_id_type=MESH)

    @pl.when(even)
    def _():
        greet(2)
        greet(-2)

    @pl.when(jnp.logical_not(even))
    def _():
        greet(turn - 3 + (turn - 1) // 2 * 2)
        greet(1)
        greet(-1)

    for d in range(1, 16):
        pl.semaphore_signal(barrier, inc=1, device_id={"ctx": (c + d) % 16}, device_id_type=MESH)
    for d in range(1, 4):
        pl.semaphore_signal(barrier, inc=1, device_id={"dp": grp * 4 + (lane_z + d) % 4}, device_id_type=MESH)
    pl.semaphore_signal(barrier, inc=1, device_id={"tp": 1 - core}, device_id_type=MESH)

    for load in first:
        load.wait()
    flat = jnp.concatenate(
        [ids_ref[...].astype(F32), probs_ref[...].astype(F32), jnp.zeros((4, 4), F32)], axis=0
    )
    flat = jnp.concatenate([flat, jnp.zeros((8, META - 4), F32)], axis=1)
    side = jnp.transpose(flat)[:4, :]
    side = jnp.concatenate([side, jnp.zeros((4, META - 8), F32)], axis=1).astype(BF16)
    for q in range(4):
        mine[q, :, :QUARTER] = cot_ref[:, QUARTER * q:QUARTER * q + QUARTER]
        mine[q, :, QUARTER:] = side
    tok[c] = mine[x]

    pl.semaphore_wait(barrier, jnp.where(even, 21, 22))

    @pl.when(turn != 2)
    def _():
        target = jnp.where(turn == 0, -2, turn - 2)
        pl.semaphore_signal(vouched, inc=1, device_id=plane(target), device_id_type=MESH)

    def a_copy(d):
        to_x, to_y = (x + d // 4) % 4, (y + d % 4) % 4
        return pltpu.make_async_remote_copy(
            src_ref=mine.at[to_x], dst_ref=tok.at[c],
            send_sem=a_send.at[d - 1], recv_sem=a_recv.at[d - 1],
            device_id={"ctx": to_x * 4 + to_y}, device_id_type=MESH,
        )

    for d in (10, 6, 14, 9, 11, 2, 8, 5, 7, 13, 15, 1, 3, 4, 12):
        a_copy(d).start()

    def factors(n, carry):
        g, u = gate[n].reshape(128, HID).astype(F32), up[n].reshape(128, HID).astype(F32)
        s = jax.nn.sigmoid(g)
        silu = g * s
        f_up[n] = silu
        f_gate[n] = u * s * (1.0 + g * (1.0 - s))
        act_t[n] = jnp.transpose(silu * u).astype(BF16)
        return carry

    for load in loads:
        load.wait()
    lax.fori_loop(0, 4, factors, 0)

    for d in range(1, 16):
        a_copy(d).wait_recv()

    for n in range(16):
        tok32[4 * n:4 * n + 4, :] = tok[n].astype(F32)
    side = tok32[:, QUARTER:]
    lanes = lax.broadcasted_iota(jnp.int32, (64, META), 1)
    expert = (mate + 4 * (lanes // 32)).astype(F32)
    hit0, hit1 = side[:, 0:1] == expert, side[:, 1:2] == expert
    weight = jnp.where(hit0, side[:, 2:3], jnp.where(hit1, side[:, 3:4], 0.0))
    hit = jnp.where(hit0 | hit1, 1.0, 0.0)
    before = (
        lax.broadcasted_iota(jnp.int32, (64, 64), 0) > lax.broadcasted_iota(jnp.int32, (64, 64), 1)
    )
    slot = jnp.dot(
        jnp.where(before, 1.0, 0.0).astype(BF16), hit.astype(BF16), preferred_element_type=F32
    )
    place = jnp.where((slot == (lanes % 32).astype(F32)) & (hit > 0.5), weight, 0.0)
    place = jnp.transpose(place)[:64, :].astype(BF16)
    made = jnp.dot(place, tok32[:, :QUARTER].astype(BF16), preferred_element_type=F32).astype(BF16)
    block[...] = made.reshape(2, 2, 16, QUARTER)

    def b_copy(s, arrives):
        return pltpu.make_async_remote_copy(
            src_ref=block.at[s], dst_ref=rows.at[x, grp, 0],
            send_sem=b_send.at[s], recv_sem=b_recv.at[arrives],
            device_id={"dp": (mate + 4 * s) * 4 + lane_z}, device_id_type=MESH,
        )

    def far(s):
        off = (mate + 4 * s - grp + 8) % 8
        return (off >= 3) & (off <= 5)

    for s in range(2):
        @pl.when(to_other(s) & jnp.logical_not(far(s)))
        def _():
            b_copy(s, self_half).start()

    @pl.when(turn != 2)
    def _():
        pl.semaphore_wait(vouched, 1)

    for s in range(2):
        @pl.when(far(s))
        def _():
            b_copy(s, self_half).start()

    for s in range(2):
        @pl.when(jnp.logical_not(to_other(s)))
        def _():
            rows[x, grp, 0] = block[s]

    def z_copy(s, d):
        return pltpu.make_async_remote_copy(
            src_ref=rows.at[x, mate + 4 * s, 0], dst_ref=rows.at[x, mate + 4 * s, 4 - d],
            send_sem=z_send.at[s, d - 1], recv_sem=z_recv.at[s, d - 1],
            device_id={"dp": grp * 4 + (lane_z + d) % 4}, device_id_type=MESH,
        )

    lax.fori_loop(4, 8, factors, 0)
    gd_acc[...] = jnp.zeros_like(gd_acc)
    dact[0:4] = jnp.zeros((4, 128, HID), F32)
    for d in range(1, 16):
        a_copy(d).wait_send()

    pos = ((x, y), (y, x))
    STEP = (1, -1)
    BOTH = (0, 1)

    def near(v, step):
        return (v + 4 + step) % 4

    def nth(n):
        return jnp.where(n < 2, -n, n - 1)

    def xy_copy(t, half, p, q, part, sems, to_p, to_q):
        xx, yy = (p, q) if half == 0 else (q, p)
        to_x, to_y = (to_p, to_q) if half == 0 else (to_q, to_p)
        cut = {None: pl.ds(0, 2), 0: pl.ds(0, 1), 1: pl.ds(1, 1)}[part]
        ref = rows.at[xx, (yy - grp + 8) % 4 + 4 * half, (pl.ds(0, 1), pl.ds(1, 3))[t], cut]
        return pltpu.make_async_remote_copy(
            src_ref=ref, dst_ref=ref, send_sem=sems[0], recv_sem=sems[1],
            device_id={"ctx": to_x * 4 + to_y}, device_id_type=MESH,
        )

    def s1(t, half, side, whose, to):
        q = pos[half][1]
        sems = (s1_send.at[t, half, side], s1_recv.at[t, half, side])
        return xy_copy(t, half, whose, q, None, sems, to, q)

    def s1f(t, half, side, whose, to):
        q = pos[half][1]
        sems = (s1f_send.at[t, half, side], s1f_recv.at[t, half, side])
        return xy_copy(t, half, whose, q, side, sems, to, q)

    def s2(t, half, n, side, whose, to):
        p = pos[half][0]
        sems = (s2_send.at[t, half, n, side], s2_recv.at[t, half, n, side])
        return xy_copy(t, half, near(p, nth(n)), whose, None, sems, p, to)

    def s2f(t, half, n, side, whose, to):
        p = pos[half][0]
        sems = (s2f_send.at[t, half, n, side], s2f_recv.at[t, half, n, side])
        return xy_copy(t, half, near(p, nth(n)), whose, side, sems, p, to)

    def start_s1(t):
        for side in BOTH:
            for half in BOTH:
                p = pos[half][0]
                s1(t, half, side, p, near(p, STEP[side])).start()

    def start_s2(t, n):
        for side in BOTH:
            for half in BOTH:
                q = pos[half][1]
                s2(t, half, n, side, q, near(q, STEP[side])).start()

    def pass_s1(t):
        for side in BOTH:
            for half in BOTH:
                p = pos[half][0]
                s1(t, half, side, near(p, -STEP[side]), p).wait_recv()
                s1f(t, half, side, near(p, -STEP[side]), near(p, STEP[side])).start()
        start_s2(t, 1)
        start_s2(t, 2)

    def end_s1(t):
        for half in BOTH:
            p = pos[half][0]
            for side in BOTH:
                s1f(t, half, side, near(p, -2 * STEP[side]), p).wait_recv()
        start_s2(t, 3)

    def pass_s2(t, n):
        for side in BOTH:
            for half in BOTH:
                q = pos[half][1]
                s2(t, half, n, side, near(q, -STEP[side]), q).wait_recv()
                s2f(t, half, n, side, near(q, -STEP[side]), near(q, STEP[side])).start()

    def end_s2(half, n):
        q = pos[half][1]
        for t in BOTH:
            for side in BOTH:
                s2f(t, half, n, side, near(q, -2 * STEP[side]), q).wait_recv()

    def t_copy(n):
        slab = dact.at[n]
        return pltpu.make_async_remote_copy(
            src_ref=slab, dst_ref=other.at[n],
            send_sem=t_send.at[n], recv_sem=t_recv.at[n],
            device_id={"tp": 1 - core}, device_id_type=MESH,
        )

    def use0(n):
        q = near(x, nth(n))
        got = rows[q, 0:4].reshape(512, QUARTER)
        part = lax.dot_general(got, w[q], (((1,), (1,)), ((), ())), preferred_element_type=F32)
        part = part.reshape(4, 128, HID)
        dact[0:4] += part
        total = gd_acc[q]
        for m in range(4):
            total += jnp.dot(act_t[m], got[128 * m:128 * m + 128], preferred_element_type=F32)
        gd_acc[q] = total

    def use1(n):
        m = (near(y, nth(n)) - grp + 8) % 4 + 4
        total = jnp.zeros((128, HID), F32)
        for q in range(4):
            got = rows[q, m].reshape(128, QUARTER)
            total += lax.dot_general(got, w[q], (((1,), (1,)), ((), ())), preferred_element_type=F32)
            gd_acc[q] += jnp.dot(act_t[m], got, preferred_element_type=F32)
        dact[m] = total
        t_copy(m).start()

    def finish(m):
        t_copy(m).wait_recv()
        total = dact[m] + other[m]
        for ref, factor in ((gg_ref, f_gate), (gu_ref, f_up)):
            value = (total * factor[m]).astype(BF16)
            for r in range(4):
                ref[m, (lane_z + r) % 4] = value[32 * r:32 * r + 32]

    def block_of(n):
        return (near(y, nth(n)) - grp + 8) % 4 + 4

    for s in BOTH:
        @pl.when(to_other(s))
        def _():
            b_copy(s, s).wait_recv()
        for d in range(1, 4):
            z_copy(s, d).start()
    start_s1(0)
    start_s2(0, 0)
    pass_s1(0)
    pass_s2(0, 0)
    for s in BOTH:
        for d in range(1, 4):
            z_copy(s, d).wait_recv()
    start_s1(1)
    end_s1(0)
    start_s2(1, 0)
    pass_s2(0, 1)
    pass_s2(0, 2)
    pass_s1(1)
    pass_s2(0, 3)
    end_s1(1)
    pass_s2(1, 0)
    pass_s2(1, 1)
    pass_s2(1, 2)
    pass_s2(1, 3)

    def use(n, carry):
        end_s2(0, n)
        use0(n)

        @pl.when(n == 3)
        def _():
            for m in range(4):
                t_copy(m).start()

        end_s2(1, n)
        use1(n)
        return carry

    lax.fori_loop(0, 4, use, 0)

    for q in range(4):
        gd_ref[:, QUARTER * q:QUARTER * q + QUARTER] = gd_acc[q].astype(BF16)
    for s in BOTH:
        @pl.when(to_other(s))
        def _():
            b_copy(s, self_half).wait_send()
        for d in range(1, 4):
            z_copy(s, d).wait_send()
    for half in BOTH:
        p, q = pos[half]
        for t in BOTH:
            for side in BOTH:
                s1(t, half, side, p, near(p, STEP[side])).wait_send()
                s1f(t, half, side, near(p, -STEP[side]), near(p, STEP[side])).wait_send()

        def left(n, carry):
            for t in BOTH:
                for side in BOTH:
                    s2(t, half, n, side, q, near(q, STEP[side])).wait_send()
                    s2f(t, half, n, side, near(q, -STEP[side]), near(q, STEP[side])).wait_send()
            return carry

        lax.fori_loop(0, 4, left, 0)

    def end(n, carry):
        finish(jnp.where(n < 3, block_of(n), jnp.where(n < 7, n - 3, block_of(3))))
        return carry

    lax.fori_loop(0, 8, end, 0)
    for n in range(8):
        t_copy(n).wait_send()


def write_out(gg_ref, gu_ref, gd_ref, gg_out, gu_out, gd_out, sem):
    copies = []
    for src, dst, amount in ((gg_ref, gg_out, 256), (gu_ref, gu_out, 256), (gd_ref, gd_out, 64)):
        for m in range(4):
            cut = pl.ds(m * amount, amount)
            copies.append(pltpu.make_async_copy(src.at[cut], dst.at[cut], sem.at[len(copies)]))
    for copy in copies:
        copy.start()
    for copy in copies:
        copy.wait()


def body(cotangent, expert_ids, route_probs, saved_gate, saved_up, down_weight):
    slabs, parts = (8, 128, HID), (8, 4, 32, HID)
    vmem, hbm, any_ = (pl.BlockSpec(memory_space=m) for m in (pltpu.VMEM, pltpu.HBM, pl.ANY))
    dma = pltpu.SemaphoreType.DMA
    gg, gu, gd = pl.pallas_call(
        kernel,
        out_shape=(
            jax.ShapeDtypeStruct(parts, BF16),
            jax.ShapeDtypeStruct(parts, BF16),
            jax.ShapeDtypeStruct((HID, D), BF16),
        ),
        in_specs=[hbm] * 6,
        out_specs=(vmem, vmem, vmem),
        scratch_shapes=[
            pltpu.VMEM((4, D), BF16),
            pltpu.VMEM((2, 4), jnp.int32),
            pltpu.VMEM((2, 4), BF16),
            pltpu.VMEM((4, 4, QUARTER + META), BF16),
            pltpu.VMEM((16, 4, QUARTER + META), BF16),
            pltpu.VMEM((64, QUARTER + META), F32),
            pltpu.VMEM((2, 2, 16, QUARTER), BF16),
            pltpu.VMEM((4, 8, 4, 2, 16, QUARTER), BF16),
            pltpu.VMEM(parts, BF16),
            pltpu.VMEM(parts, BF16),
            pltpu.VMEM((4, HID, QUARTER), BF16),
            pltpu.VMEM(slabs, F32),
            pltpu.VMEM(slabs, F32),
            pltpu.VMEM((8, HID, 128), BF16),
            pltpu.VMEM(slabs, F32),
            pltpu.VMEM(slabs, F32),
            pltpu.VMEM((4, HID, QUARTER), F32),
            dma((15,)), pltpu.SemaphoreType.REGULAR, dma((15,)), dma((15,)), dma((2,)), dma((2,)), dma((2, 3)), dma((2, 3)),
            dma((2, 2, 2)), dma((2, 2, 2)), dma((2, 2, 2)), dma((2, 2, 2)),
            dma((2, 2, 4, 2)), dma((2, 2, 4, 2)), dma((2, 2, 4, 2)), dma((2, 2, 4, 2)),
            dma((8,)), dma((8,)),
        ],
        compiler_params=pltpu.CompilerParams(
            collective_id=0, has_side_effects=True, vmem_limit_bytes=40 * 1024 * 1024
        ),
    )(
        *(
            pltpu.with_memory_space_constraint(a, pltpu.HBM)
            for a in (
                cotangent, expert_ids.T, route_probs.T,
                saved_gate.reshape(parts), saved_up.reshape(parts), down_weight,
            )
        ),
    )
    return pl.pallas_call(
        write_out,
        out_shape=(
            jax.ShapeDtypeStruct((1024, HID), BF16),
            jax.ShapeDtypeStruct((1024, HID), BF16),
            jax.ShapeDtypeStruct((HID, D), BF16),
        ),
        in_specs=[vmem] * 3,
        out_specs=(any_,) * 3,
        scratch_shapes=[dma((12,))],
        compiler_params=pltpu.CompilerParams(vmem_limit_bytes=4 * 1024 * 1024),
    )(gg.reshape(1024, HID), gu.reshape(1024, HID), gd)


def solution(mesh):
    return jax.shard_map(
        body,
        mesh=mesh,
        in_specs=(
            P(("dp", "ctx"), "tp"),
            P(("dp", "ctx"), None),
            P(("dp", "ctx"), None),
            P(None, ("dp", "ctx")),
            P(None, ("dp", "ctx")),
            P(("dp", "ctx"), "tp"),
        ),
        out_specs=(P(None, ("dp", "ctx")), P(None, ("dp", "ctx")), P(("dp", "ctx"), "tp")),
        check_vma=False,
    )
```

```python
import jax
import jax.numpy as jnp
from jax import lax
from jax.experimental import pallas as pl
from jax.experimental.pallas import tpu as pltpu
from jax.sharding import PartitionSpec as P

D = 1536
QUARTER = D // 4
HID = 256
META = 128
MESH = pl.DeviceIdType.MESH
F32 = jnp.float32
BF16 = jnp.bfloat16


def kernel(
    cot_hbm, ids_hbm, probs_hbm, gate_hbm, up_hbm, w_hbm,
    gg_ref, gu_ref, gd_ref,
    cot_ref, ids_ref, probs_ref, mine, tok, tok32, block, rows, gate, up, w, f_gate, f_up, act0, act1, w_t, dact, other, gd_acc,
    load_sem, vouched, a_send, a_recv, b_send, b_recv, z_send, z_recv,
    s1_send, s1_recv, s1f_send, s1f_recv, s2_send, s2_recv, s2f_send, s2f_recv,
    t_send, t_recv,
):
    z, c, core = lax.axis_index("dp"), lax.axis_index("ctx"), lax.axis_index("tp")
    x, y = c // 4, c % 4
    grp, lane_z = z // 4, z % 4
    mate = (y - grp + 8) % 4
    self_half = grp // 4
    alone = mate == grp % 4

    def to_other(s):
        return jnp.logical_not(alone & (self_half == s))

    first = [
        pltpu.make_async_copy(src, dst, load_sem.at[12 + n])
        for n, (src, dst) in enumerate(((cot_hbm, cot_ref), (ids_hbm, ids_ref), (probs_hbm, probs_ref)))
    ]
    for load in first:
        load.start()
    loads = []
    for src, dst in ((gate_hbm, gate), (up_hbm, up)):
        for r in range(4):
            loads.append((src.at[:, (lane_z + r) % 4], dst.at[:, r]))
    for m in range(4):
        loads.append((w_hbm.at[:, pl.ds(QUARTER * m, QUARTER)], w.at[m]))
    loads = [pltpu.make_async_copy(src, dst, load_sem.at[n]) for n, (src, dst) in enumerate(loads)]
    for load in loads:
        load.start()

    barrier = pltpu.get_barrier_semaphore()
    turn = (y - 2 * grp + 16) % 4
    even = turn % 2 == 0

    def plane(off):
        return {"dp": (grp + off + 8) % 8 * 4 + lane_z}

    def greet(off):
        pl.semaphore_signal(barrier, inc=1, device_id=plane(off), device_id_type=MESH)

    @pl.when(even)
    def _():
        greet(2)
        greet(-2)

    @pl.when(jnp.logical_not(even))
    def _():
        greet(turn - 3 + (turn - 1) // 2 * 2)
        greet(1)
        greet(-1)

    for d in range(1, 16):
        pl.semaphore_signal(barrier, inc=1, device_id={"ctx": (c + d) % 16}, device_id_type=MESH)
    for d in range(1, 4):
        pl.semaphore_signal(barrier, inc=1, device_id={"dp": grp * 4 + (lane_z + d) % 4}, device_id_type=MESH)
    pl.semaphore_signal(barrier, inc=1, device_id={"tp": 1 - core}, device_id_type=MESH)

    for load in first:
        load.wait()
    flat = jnp.concatenate(
        [ids_ref[...].astype(F32), probs_ref[...].astype(F32), jnp.zeros((4, 4), F32)], axis=0
    )
    flat = jnp.concatenate([flat, jnp.zeros((8, META - 4), F32)], axis=1)
    side = jnp.transpose(flat)[:4, :]
    side = jnp.concatenate([side, jnp.zeros((4, META - 8), F32)], axis=1).astype(BF16)
    for q in range(4):
        mine[q, :, :QUARTER] = cot_ref[:, QUARTER * q:QUARTER * q + QUARTER]
        mine[q, :, QUARTER:] = side
    tok[c] = mine[x]

    pl.semaphore_wait(barrier, jnp.where(even, 21, 22))

    @pl.when(turn != 2)
    def _():
        target = jnp.where(turn == 0, -2, turn - 2)
        pl.semaphore_signal(vouched, inc=1, device_id=plane(target), device_id_type=MESH)

    def a_copy(d):
        to_x, to_y = (x + d // 4) % 4, (y + d % 4) % 4
        return pltpu.make_async_remote_copy(
            src_ref=mine.at[to_x], dst_ref=tok.at[c],
            send_sem=a_send.at[d - 1], recv_sem=a_recv.at[d - 1],
            device_id={"ctx": to_x * 4 + to_y}, device_id_type=MESH,
        )

    for d in (10, 6, 14, 9, 11, 2, 8, 5, 7, 13, 15, 1, 3, 4, 12):
        a_copy(d).start()

    def factors(n):
        g, u = gate[n].reshape(128, HID).astype(F32), up[n].reshape(128, HID).astype(F32)
        s = jax.nn.sigmoid(g)
        silu = g * s
        f_up[n] = silu
        f_gate[n] = u * s * (1.0 + g * (1.0 - s))
        return jnp.transpose(silu * u).astype(BF16)

    def factors0(n, carry):
        act0[:, pl.ds(pl.multiple_of(n * 128, 128), 128)] = factors(n)
        return carry

    def factors1(n, carry):
        act1[n - 4] = factors(n)
        return carry

    for load in loads:
        load.wait()
    lax.fori_loop(0, 4, factors0, 0)

    for d in range(1, 16):
        a_copy(d).wait_recv()

    for n in range(16):
        tok32[4 * n:4 * n + 4, :] = tok[n].astype(F32)
    side = tok32[:, QUARTER:]
    lanes = lax.broadcasted_iota(jnp.int32, (64, META), 1)
    expert = (mate + 4 * (lanes // 32)).astype(F32)
    hit0, hit1 = side[:, 0:1] == expert, side[:, 1:2] == expert
    weight = jnp.where(hit0, side[:, 2:3], jnp.where(hit1, side[:, 3:4], 0.0))
    hit = jnp.where(hit0 | hit1, 1.0, 0.0)
    before = (
        lax.broadcasted_iota(jnp.int32, (64, 64), 0) > lax.broadcasted_iota(jnp.int32, (64, 64), 1)
    )
    slot = jnp.dot(
        jnp.where(before, 1.0, 0.0).astype(BF16), hit.astype(BF16), preferred_element_type=F32
    )
    place = jnp.where((slot == (lanes % 32).astype(F32)) & (hit > 0.5), weight, 0.0)
    place = jnp.transpose(place)[:64, :].astype(BF16)
    made = jnp.dot(place, tok32[:, :QUARTER].astype(BF16), preferred_element_type=F32).astype(BF16)
    block[...] = made.reshape(2, 2, 16, QUARTER)

    def b_copy(s, arrives):
        return pltpu.make_async_remote_copy(
            src_ref=block.at[s], dst_ref=rows.at[x, grp, 0],
            send_sem=b_send.at[s], recv_sem=b_recv.at[arrives],
            device_id={"dp": (mate + 4 * s) * 4 + lane_z}, device_id_type=MESH,
        )

    def far(s):
        off = (mate + 4 * s - grp + 8) % 8
        return (off >= 3) & (off <= 5)

    for s in range(2):
        @pl.when(to_other(s) & jnp.logical_not(far(s)))
        def _():
            b_copy(s, self_half).start()

    @pl.when(turn != 2)
    def _():
        pl.semaphore_wait(vouched, 1)

    for s in range(2):
        @pl.when(far(s))
        def _():
            b_copy(s, self_half).start()

    for s in range(2):
        @pl.when(jnp.logical_not(to_other(s)))
        def _():
            rows[x, grp, 0] = block[s]

    def z_copy(s, d):
        return pltpu.make_async_remote_copy(
            src_ref=rows.at[x, mate + 4 * s, 0], dst_ref=rows.at[x, mate + 4 * s, 4 - d],
            send_sem=z_send.at[s, d - 1], recv_sem=z_recv.at[s, d - 1],
            device_id={"dp": grp * 4 + (lane_z + d) % 4}, device_id_type=MESH,
        )

    lax.fori_loop(4, 8, factors1, 0)
    for q in range(4):
        w_t[q] = jnp.transpose(w[q].astype(F32)).astype(BF16)
    gd_acc[...] = jnp.zeros_like(gd_acc)
    dact[0:4] = jnp.zeros((4, 128, HID), F32)
    for d in range(1, 16):
        a_copy(d).wait_send()

    pos = ((x, y), (y, x))
    STEP = (1, -1)
    BOTH = (0, 1)

    def near(v, step):
        return (v + 4 + step) % 4

    def nth(n):
        return jnp.where(n < 2, -n, n - 1)

    def xy_copy(t, half, p, q, part, sems, to_p, to_q):
        xx, yy = (p, q) if half == 0 else (q, p)
        to_x, to_y = (to_p, to_q) if half == 0 else (to_q, to_p)
        cut = {None: pl.ds(0, 2), 0: pl.ds(0, 1), 1: pl.ds(1, 1)}[part]
        ref = rows.at[xx, (yy - grp + 8) % 4 + 4 * half, (pl.ds(0, 1), pl.ds(1, 3))[t], cut]
        return pltpu.make_async_remote_copy(
            src_ref=ref, dst_ref=ref, send_sem=sems[0], recv_sem=sems[1],
            device_id={"ctx": to_x * 4 + to_y}, device_id_type=MESH,
        )

    def s1(t, half, side, whose, to):
        q = pos[half][1]
        sems = (s1_send.at[t, half, side], s1_recv.at[t, half, side])
        return xy_copy(t, half, whose, q, None, sems, to, q)

    def s1f(t, half, side, whose, to):
        q = pos[half][1]
        sems = (s1f_send.at[t, half, side], s1f_recv.at[t, half, side])
        return xy_copy(t, half, whose, q, side, sems, to, q)

    def s2(t, half, n, side, whose, to):
        p = pos[half][0]
        sems = (s2_send.at[t, half, n, side], s2_recv.at[t, half, n, side])
        return xy_copy(t, half, near(p, nth(n)), whose, None, sems, p, to)

    def s2f(t, half, n, side, whose, to):
        p = pos[half][0]
        sems = (s2f_send.at[t, half, n, side], s2f_recv.at[t, half, n, side])
        return xy_copy(t, half, near(p, nth(n)), whose, side, sems, p, to)

    def start_s1(t):
        for side in BOTH:
            for half in BOTH:
                p = pos[half][0]
                s1(t, half, side, p, near(p, STEP[side])).start()

    def start_s2(t, n):
        for side in BOTH:
            for half in BOTH:
                q = pos[half][1]
                s2(t, half, n, side, q, near(q, STEP[side])).start()

    def pass_s1(t):
        for side in BOTH:
            for half in BOTH:
                p = pos[half][0]
                s1(t, half, side, near(p, -STEP[side]), p).wait_recv()
                s1f(t, half, side, near(p, -STEP[side]), near(p, STEP[side])).start()
        start_s2(t, 1)
        start_s2(t, 2)

    def end_s1(t):
        for half in BOTH:
            p = pos[half][0]
            for side in BOTH:
                s1f(t, half, side, near(p, -2 * STEP[side]), p).wait_recv()
        start_s2(t, 3)

    def pass_s2(t, n):
        for side in BOTH:
            for half in BOTH:
                q = pos[half][1]
                s2(t, half, n, side, near(q, -STEP[side]), q).wait_recv()
                s2f(t, half, n, side, near(q, -STEP[side]), near(q, STEP[side])).start()

    def end_s2(half, n):
        q = pos[half][1]
        for t in BOTH:
            for side in BOTH:
                s2f(t, half, n, side, near(q, -2 * STEP[side]), q).wait_recv()

    def t_copy(n):
        slab = dact.at[n]
        return pltpu.make_async_remote_copy(
            src_ref=slab, dst_ref=other.at[n],
            send_sem=t_send.at[n], recv_sem=t_recv.at[n],
            device_id={"tp": 1 - core}, device_id_type=MESH,
        )

    def use0(n):
        q = near(x, nth(n))
        got = rows[q, 0:4].reshape(512, QUARTER)
        part = jnp.dot(got, w_t[q], preferred_element_type=F32)
        part = part.reshape(4, 128, HID)
        dact[0:4] += part
        gd_acc[q] += jnp.dot(act0[...], got, preferred_element_type=F32)

    def use1(n):
        m = (near(y, nth(n)) - grp + 8) % 4 + 4
        total = jnp.zeros((128, HID), F32)
        for q in range(4):
            got = rows[q, m].reshape(128, QUARTER)
            total += jnp.dot(got, w_t[q], preferred_element_type=F32)
            gd_acc[q] += jnp.dot(act1[m - 4], got, preferred_element_type=F32)
        dact[m] = total
        t_copy(m).start()

    def finish(m):
        t_copy(m).wait_recv()
        total = dact[m] + other[m]
        for ref, factor in ((gg_ref, f_gate), (gu_ref, f_up)):
            value = (total * factor[m]).astype(BF16)
            for r in range(4):
                ref[m, (lane_z + r) % 4] = value[32 * r:32 * r + 32]

    def block_of(n):
        return (near(y, nth(n)) - grp + 8) % 4 + 4

    for s in BOTH:
        @pl.when(to_other(s))
        def _():
            b_copy(s, s).wait_recv()
        for d in range(1, 4):
            z_copy(s, d).start()
    start_s1(0)
    start_s2(0, 0)
    pass_s1(0)
    pass_s2(0, 0)
    for s in BOTH:
        for d in range(1, 4):
            z_copy(s, d).wait_recv()
    start_s1(1)
    end_s1(0)
    start_s2(1, 0)
    pass_s2(0, 1)
    pass_s2(0, 2)
    pass_s1(1)
    pass_s2(0, 3)
    end_s1(1)
    pass_s2(1, 0)
    pass_s2(1, 1)
    pass_s2(1, 2)
    pass_s2(1, 3)

    def use(n, carry):
        end_s2(0, n)
        use0(n)

        @pl.when(n == 3)
        def _():
            for m in range(4):
                t_copy(m).start()

        end_s2(1, n)
        use1(n)
        return carry

    lax.fori_loop(0, 4, use, 0)

    for q in range(4):
        gd_ref[:, QUARTER * q:QUARTER * q + QUARTER] = gd_acc[q].astype(BF16)
    for s in BOTH:
        @pl.when(to_other(s))
        def _():
            b_copy(s, self_half).wait_send()
        for d in range(1, 4):
            z_copy(s, d).wait_send()
    for half in BOTH:
        p, q = pos[half]
        for t in BOTH:
            for side in BOTH:
                s1(t, half, side, p, near(p, STEP[side])).wait_send()
                s1f(t, half, side, near(p, -STEP[side]), near(p, STEP[side])).wait_send()

        def left(n, carry):
            for t in BOTH:
                for side in BOTH:
                    s2(t, half, n, side, q, near(q, STEP[side])).wait_send()
                    s2f(t, half, n, side, near(q, -STEP[side]), near(q, STEP[side])).wait_send()
            return carry

        lax.fori_loop(0, 4, left, 0)

    def end(n, carry):
        finish(jnp.where(n < 3, block_of(n), jnp.where(n < 7, n - 3, block_of(3))))
        return carry

    lax.fori_loop(0, 8, end, 0)
    for n in range(8):
        t_copy(n).wait_send()


def write_out(gg_ref, gu_ref, gd_ref, gg_out, gu_out, gd_out, sem):
    copies = []
    for src, dst, amount in ((gg_ref, gg_out, 256), (gu_ref, gu_out, 256), (gd_ref, gd_out, 64)):
        for m in range(4):
            cut = pl.ds(m * amount, amount)
            copies.append(pltpu.make_async_copy(src.at[cut], dst.at[cut], sem.at[len(copies)]))
    for copy in copies:
        copy.start()
    for copy in copies:
        copy.wait()


def body(cotangent, expert_ids, route_probs, saved_gate, saved_up, down_weight):
    slabs, parts = (8, 128, HID), (8, 4, 32, HID)
    vmem, hbm, any_ = (pl.BlockSpec(memory_space=m) for m in (pltpu.VMEM, pltpu.HBM, pl.ANY))
    dma = pltpu.SemaphoreType.DMA
    gg, gu, gd = pl.pallas_call(
        kernel,
        out_shape=(
            jax.ShapeDtypeStruct(parts, BF16),
            jax.ShapeDtypeStruct(parts, BF16),
            jax.ShapeDtypeStruct((HID, D), BF16),
        ),
        in_specs=[hbm] * 6,
        out_specs=(vmem, vmem, vmem),
        scratch_shapes=[
            pltpu.VMEM((4, D), BF16),
            pltpu.VMEM((2, 4), jnp.int32),
            pltpu.VMEM((2, 4), BF16),
            pltpu.VMEM((4, 4, QUARTER + META), BF16),
            pltpu.VMEM((16, 4, QUARTER + META), BF16),
            pltpu.VMEM((64, QUARTER + META), F32),
            pltpu.VMEM((2, 2, 16, QUARTER), BF16),
            pltpu.VMEM((4, 8, 4, 2, 16, QUARTER), BF16),
            pltpu.VMEM(parts, BF16),
            pltpu.VMEM(parts, BF16),
            pltpu.VMEM((4, HID, QUARTER), BF16),
            pltpu.VMEM(slabs, F32),
            pltpu.VMEM(slabs, F32),
            pltpu.VMEM((HID, 512), BF16),
            pltpu.VMEM((4, HID, 128), BF16),
            pltpu.VMEM((4, QUARTER, HID), BF16),
            pltpu.VMEM(slabs, F32),
            pltpu.VMEM(slabs, F32),
            pltpu.VMEM((4, HID, QUARTER), F32),
            dma((15,)), pltpu.SemaphoreType.REGULAR, dma((15,)), dma((15,)), dma((2,)), dma((2,)), dma((2, 3)), dma((2, 3)),
            dma((2, 2, 2)), dma((2, 2, 2)), dma((2, 2, 2)), dma((2, 2, 2)),
            dma((2, 2, 4, 2)), dma((2, 2, 4, 2)), dma((2, 2, 4, 2)), dma((2, 2, 4, 2)),
            dma((8,)), dma((8,)),
        ],
        compiler_params=pltpu.CompilerParams(
            collective_id=0, has_side_effects=True, vmem_limit_bytes=40 * 1024 * 1024
        ),
    )(
        *(
            pltpu.with_memory_space_constraint(a, pltpu.HBM)
            for a in (
                cotangent, expert_ids.T, route_probs.T,
                saved_gate.reshape(parts), saved_up.reshape(parts), down_weight,
            )
        ),
    )
    return pl.pallas_call(
        write_out,
        out_shape=(
            jax.ShapeDtypeStruct((1024, HID), BF16),
            jax.ShapeDtypeStruct((1024, HID), BF16),
            jax.ShapeDtypeStruct((HID, D), BF16),
        ),
        in_specs=[vmem] * 3,
        out_specs=(any_,) * 3,
        scratch_shapes=[dma((12,))],
        compiler_params=pltpu.CompilerParams(vmem_limit_bytes=4 * 1024 * 1024),
    )(gg.reshape(1024, HID), gu.reshape(1024, HID), gd)


def solution(mesh):
    return jax.shard_map(
        body,
        mesh=mesh,
        in_specs=(
            P(("dp", "ctx"), "tp"),
            P(("dp", "ctx"), None),
            P(("dp", "ctx"), None),
            P(None, ("dp", "ctx")),
            P(None, ("dp", "ctx")),
            P(("dp", "ctx"), "tp"),
        ),
        out_specs=(P(None, ("dp", "ctx")), P(None, ("dp", "ctx")), P(("dp", "ctx"), "tp")),
        check_vma=False,
    )
```
